512 devices in a mesh: ctx: 8 (over z_hi, core), grp: 64 (over y, x, z_lo).
Axes of the slice: x: 4, y: 4, z: 16 (z_hi: 4, z_lo: 4; z = z_hi * 4 + z_lo), core: 2. Of those that a mesh axis runs over, the one named last changes fastest.
Arguments:
- queries: bfloat16 [128, 4096, 576], P('grp', 'ctx'), may hold values from -32 to 32
- kv_latent: bfloat16 [4096, 576], P(('ctx', 'grp')), may hold values from -8 to 8
- vert_tiles: int32 [64, 6], replicated, may hold values from 0 to 31
- slash_offsets: int32 [64, 4], replicated, may hold values from 1 to 31
- w_uv: bfloat16 [128, 512, 128], P('grp'), may hold values from -0.25 to 0.25
Outputs:
- attended: bfloat16 [128, 4096, 128], P('grp', 'ctx')
The draws below stay inside these ranges and needn't reach their ends.
All inputs are finite; a program needn't handle non-finite values.
Results may differ from the reference program's by a relative error of at most 0.0055.
Values may be sent and summed in bfloat16 or wider, within the bound.
No kernel may reach another device: no remote copies, remote signals or barrier semaphores. Data moves between devices by JAX's collectives and lax.ppermute only.
A program may use at most 64 MiB of HBM per device.

```python
import jax
import jax.numpy as jnp
from jax import lax

LAT = 512
VDIM = 128
KV = 576
HEAD_DEV = 2
HEADS = 128
GROUPS = 64
TILE = 128
LENGTH = 4096
TILES = 32
NV = 6
NS = 4
AMAX = 11


def common_latent(key):
    return jax.random.normal(key, (LENGTH, KV), jnp.float32)


def draw_kv_latent(key, part):
    source = common_latent(key)
    return jnp.clip(source, -8.0, 8.0).astype(jnp.bfloat16)


def draw_queries(key, part):
    key = jax.random.fold_in(key, 23)
    first_key = jax.random.fold_in(key, 0)
    fresh = jax.random.normal(first_key, (HEADS, LENGTH, KV), jnp.float32)
    return jnp.clip(fresh, -32.0, 32.0).astype(jnp.bfloat16)


def plant(entries, key, low, top_value):
    spot = [jax.random.randint(jax.random.fold_in(key, axis), (), 0, length) for axis, length in enumerate(entries.shape)]
    longest = entries.shape.index(max(entries.shape))
    beside = spot[:longest] + [(spot[longest] + 1) % entries.shape[longest]] + spot[longest + 1:]
    return entries.at[tuple(spot)].set(low).at[tuple(beside)].set(top_value)


def level_of(rng, shape, cuts, low, largest):
    factor_of, own = 1.0, jax.random.fold_in(rng, 6)
    for axis_at, parts in cuts:
        heights = jnp.exp(jax.random.uniform(jax.random.fold_in(own, axis_at), (parts,), jnp.float32, low / len(cuts), largest / len(cuts)))
        factor_of = factor_of * jnp.repeat(heights, shape[axis_at] // parts).reshape([-1 if axis == axis_at else 1 for axis in range(len(shape))])
    return factor_of


def normal_values(stream_key, dims, scale, reach, cuts=(), kind=jnp.bfloat16):
    entries = jax.random.normal(stream_key, dims, jnp.float32) * scale
    if len(cuts) > 0:
        entries = level_of(stream_key, dims, cuts, -0.22, 0.18) * entries
    return jnp.clip(entries, min=-reach, max=reach).astype(kind)


def setup_inputs(seed: int = 0) -> dict:
    key_of = jax.random.split(jax.random.key(seed), 6)
    return {
        "queries": draw_queries(jax.random.fold_in(key_of[5], 71), 0),
        "kv_latent": draw_kv_latent(jax.random.fold_in(key_of[5], 71), 0),
        "vert_tiles": plant(jax.random.randint(key_of[2], (GROUPS, NV), 0, TILES), jax.random.fold_in(key_of[2], 1), 0, TILES - 1).astype(jnp.int32),
        "slash_offsets": plant(jax.random.randint(key_of[3], (GROUPS, NS), 1, TILES), jax.random.fold_in(key_of[3], 1), 1, TILES - 1).astype(jnp.int32),
        "w_uv": normal_values(key_of[4], (HEADS, LAT, VDIM), LAT ** -0.5, 0.25, ((0, 64),)),
    }


score_scale = 192.0 ** -0.5
masked_score = -1e30


def active_tiles(vert_row, slash_row, block_index):
    columns = jnp.arange(TILES, dtype=jnp.int32)
    on_vert = jnp.any(columns[:, None] == vert_row[None, :], axis=1)
    on_slash = jnp.any((block_index - columns)[:, None] == slash_row[None, :], axis=1)
    return (columns <= block_index) & ((columns == block_index) | on_vert | on_slash)


def block_latent(query_group, kv_latent, vert_row, slash_row, block_index):
    query_block = lax.dynamic_slice_in_dim(query_group, block_index * TILE, TILE, 1).astype(jnp.float32)
    tile_mask = active_tiles(vert_row, slash_row, block_index)
    live_count = jnp.sum(tile_mask.astype(jnp.int32))
    picked = jnp.nonzero(tile_mask, size=AMAX, fill_value=0)[0].astype(jnp.int32)
    tile_live = jnp.arange(AMAX, dtype=jnp.int32) < live_count
    key_rows = kv_latent.reshape(TILES, TILE, KV)[picked].reshape(AMAX * TILE, KV).astype(jnp.float32)
    key_pos = (picked[:, None] * TILE + jnp.arange(TILE, dtype=jnp.int32)[None, :]).reshape(-1)
    query_pos = block_index * TILE + jnp.arange(TILE, dtype=jnp.int32)
    allowed = jnp.repeat(tile_live, TILE)[None, :] & (key_pos[None, :] <= query_pos[:, None])
    scores = jnp.einsum("hqc,kc->hqk", query_block, key_rows) * score_scale
    scores = jnp.where(allowed[None], scores, masked_score)
    row_top = jnp.max(scores, axis=2, keepdims=True)
    weights = jnp.where(allowed[None], jnp.exp(scores - row_top), 0.0)
    row_total = jnp.sum(weights, axis=2, keepdims=True)
    rounded = lax.optimization_barrier(weights.astype(jnp.bfloat16)).astype(jnp.float32)
    latent = jnp.einsum("hqk,kc->hqc", rounded, key_rows[:, :LAT]) / row_total
    return latent.astype(jnp.bfloat16)


def group_output(query_group, kv_latent, vert_row, slash_row, weight_group):
    def one_block(block_index):
        latent = block_latent(query_group, kv_latent, vert_row, slash_row, block_index)
        projected = jnp.einsum("hqc,hcd->hqd", latent.astype(jnp.float32), weight_group.astype(jnp.float32))
        return projected.astype(jnp.bfloat16)

    pieces = lax.map(one_block, jnp.arange(TILES, dtype=jnp.int32))
    return pieces.transpose(1, 0, 2, 3).reshape(HEAD_DEV, LENGTH, VDIM)


def reference(queries, kv_latent, vert_tiles, slash_offsets, w_uv):
    grouped = queries.reshape(GROUPS, HEAD_DEV, LENGTH, KV)
    weights = w_uv.reshape(GROUPS, HEAD_DEV, LAT, VDIM)
    result = lax.map(lambda member: group_output(member[0], kv_latent, member[1], member[2], member[3]),
                     (grouped, vert_tiles, slash_offsets, weights))
    return result.reshape(HEADS, LENGTH, VDIM)
```

```python
import jax
import jax.numpy as jnp
from jax import lax
from jax.experimental import pallas as pl
from jax.experimental.pallas import tpu as pltpu
from jax.sharding import Mesh, PartitionSpec as P

TILE = 128
HEADS = 2
LAT = 512
KV = 576
ROWS = 512
BLOCKS = 4
SLOTS = 12
ROW_SCALE = 192.0 ** -0.5
DEAD = -1e30


def attend(vert, slash, place, q_ref, kv_ref, w_ref, out_ref, list_ref, s_ref):
    first = place[0] * BLOCKS
    row = lax.broadcasted_iota(jnp.int32, (HEADS * TILE, 2 * TILE), 0) & (TILE - 1)
    col = lax.broadcasted_iota(jnp.int32, (HEADS * TILE, 2 * TILE), 1)

    def keys(tile):
        zh = tile >> 3
        core = (tile >> 2) & 1
        y = tile & 3
        return kv_ref[core, y, :, zh].reshape(TILE, KV)

    for b in range(BLOCKS):
        i = first + b
        live = jnp.int32(0)
        for n in range(6):
            v = vert[n]
            live = live | jnp.where(v < i, jnp.int32(1) << v, 0)
        for n in range(4):
            v = i - slash[n]
            live = live | jnp.where(v >= 0, jnp.int32(1) << jnp.maximum(v, 0), 0)
        for n in range(1, SLOTS):
            list_ref[b, n] = i
        list_ref[b, 0] = i
        count = jnp.int32(1)
        for j in range(31):
            list_ref[b, count] = j
            count = count + ((live >> j) & 1)
        for n in range(SLOTS - 1, SLOTS):
            pass
        q = q_ref[:, b * TILE : (b + 1) * TILE, :].reshape(HEADS * TILE, KV)
        top = None
        for p in range(SLOTS // 2):
            k = jnp.concatenate([keys(list_ref[b, 2 * p]), keys(list_ref[b, 2 * p + 1])], axis=0)
            s = lax.dot_general(q, k, (((1,), (1,)), ((), ())), preferred_element_type=jnp.float32)
            s = s * ROW_SCALE
            if p == 0:
                ok = ((col < TILE) & (col <= row)) | ((col >= TILE) & (count > 1))
            else:
                ok = col < (count - 2 * p) * TILE
            s = jnp.where(ok, s, DEAD)
            s_ref[:, p * 2 * TILE : (p + 1) * 2 * TILE] = s
            t = jnp.max(s, axis=1, keepdims=True)
            top = t if top is None else jnp.maximum(top, t)
        total = jnp.zeros((HEADS * TILE, 1), jnp.float32)
        acc = jnp.zeros((HEADS * TILE, LAT), jnp.float32)
        for p in range(SLOTS // 2):
            v = jnp.concatenate([keys(list_ref[b, 2 * p]), keys(list_ref[b, 2 * p + 1])], axis=0)[:, :LAT]
            w = jnp.exp(s_ref[:, p * 2 * TILE : (p + 1) * 2 * TILE] - top)
            total = total + jnp.sum(w, axis=1, keepdims=True)
            acc = acc + jnp.dot(w.astype(jnp.bfloat16), v, preferred_element_type=jnp.float32)
        latent = (acc / total).astype(jnp.bfloat16)
        for h in range(HEADS):
            up = jnp.dot(latent[h * TILE : (h + 1) * TILE], w_ref[h], preferred_element_type=jnp.float32)
            out_ref[h, b * TILE : (b + 1) * TILE, :] = up.astype(jnp.bfloat16)


def attention(vert, slash, place, q, kv, w):
    smem = pl.BlockSpec(memory_space=pltpu.SMEM)
    vmem = pl.BlockSpec(memory_space=pltpu.VMEM)
    return pl.pallas_call(
        attend,
        out_shape=jax.ShapeDtypeStruct((HEADS, ROWS, 128), jnp.bfloat16),
        in_specs=[smem, smem, smem, vmem, vmem, vmem],
        out_specs=vmem,
        scratch_shapes=[
            pltpu.SMEM((BLOCKS, 32), jnp.int32),
            pltpu.VMEM((HEADS * TILE, SLOTS * TILE), jnp.float32),
        ],
        compiler_params=pltpu.CompilerParams(vmem_limit_bytes=40 * 1024 * 1024),
        name="attention",
    )(vert, slash, place, q, kv, w)


def on_device(queries, kv_latent, vert_tiles, slash_offsets, w_uv):
    spread = jnp.broadcast_to(kv_latent[None], (16, 8, KV))
    along = lax.all_to_all(spread, ("zh", "zl"), 0, 0)
    spread = jnp.broadcast_to(along.reshape(1, 128, KV), (16, 128, KV))
    plane = lax.all_to_all(spread, ("y", "x"), 0, 0)
    whole = lax.all_gather(plane, "core", axis=0)
    whole = whole.reshape(2, 4, 4, 4, 32, KV)
    ctx_at = lax.axis_index("zh") * 2 + lax.axis_index("core")
    grp_at = (lax.axis_index("y") * 4 + lax.axis_index("x")) * 4 + lax.axis_index("zl")
    place = jnp.reshape(ctx_at, (1,)).astype(jnp.int32)
    return attention(vert_tiles[grp_at], slash_offsets[grp_at], place, queries, whole, w_uv)


def solution(mesh):
    fine = Mesh(mesh.devices.reshape(4, 2, 4, 4, 4), ("zh", "core", "y", "x", "zl"))
    ctx, grp = ("zh", "core"), ("y", "x", "zl")
    placed = (P(grp, ctx, None), P(ctx + grp, None), P(), P(), P(grp, None, None))
    return jax.shard_map(
        on_device, mesh=fine, in_specs=placed, out_specs=P(grp, ctx, None), check_vma=False
    )
```

```python
import functools

import jax
import jax.numpy as jnp
from jax import lax
from jax.experimental import pallas as pl
from jax.experimental.pallas import tpu as pltpu
from jax.sharding import Mesh, PartitionSpec as P

TILE = 128
HEADS = 2
LAT = 512
KV = 576
WIDE = 640
ROWS = 512
BLOCKS = 4
ROW_SCALE = 192.0 ** -0.5
DEAD = -1e30
ALL = ("zh", "core", "y", "x", "zl")


def attend(slots, place, vert, slash, q_ref, kv_ref, w_ref, out_ref, list_ref, s_ref):
    first = place[0] * BLOCKS
    core = place[1]
    row = lax.broadcasted_iota(jnp.int32, (HEADS * TILE, 2 * TILE), 0) & (TILE - 1)
    col = lax.broadcasted_iota(jnp.int32, (HEADS * TILE, 2 * TILE), 1)

    def keys(tile, width):
        zh, half, y = tile >> 3, (tile >> 2) & 1, tile & 3
        side = half ^ core
        start = jnp.where(half == 0, 4 * y, y)
        step = jnp.where(half == 0, 1, 4)
        return [kv_ref[side, start + step * n, zh, :, :width] for n in range(4)]

    def pair(b, p, width):
        return jnp.concatenate(keys(list_ref[b, 2 * p], width) + keys(list_ref[b, 2 * p + 1], width), axis=0)

    for b in range(BLOCKS):
        i = first + b
        live = jnp.int32(0)
        for n in range(6):
            v = vert[n]
            live = live | jnp.where(v < i, jnp.int32(1) << v, 0)
        for n in range(4):
            v = i - slash[n]
            live = live | jnp.where(v >= 0, jnp.int32(1) << jnp.maximum(v, 0), 0)
        for n in range(slots):
            list_ref[b, n] = i
        count = jnp.int32(1)
        for j in range(min(31, slots * 4)):
            bit = (live >> j) & 1
            list_ref[b, count] = jnp.where(bit == 1, j, i)
            count = count + bit
        q = q_ref[:, b * TILE : (b + 1) * TILE, :].reshape(HEADS * TILE, KV)
        top = None
        for p in range(slots // 2):
            s = lax.dot_general(q, pair(b, p, KV), (((1,), (1,)), ((), ())), preferred_element_type=jnp.float32)
            s = s * ROW_SCALE
            if p == 0:
                ok = ((col < TILE) & (col <= row)) | ((col >= TILE) & (count > 1))
            else:
                ok = col < (count - 2 * p) * TILE
            s = jnp.where(ok, s, DEAD)
            s_ref[:, p * 2 * TILE : (p + 1) * 2 * TILE] = s
            t = jnp.max(s, axis=1, keepdims=True)
            top = t if top is None else jnp.maximum(top, t)
        total = jnp.zeros((HEADS * TILE, 1), jnp.float32)
        acc = jnp.zeros((HEADS * TILE, LAT), jnp.float32)
        for p in range(slots // 2):
            w = jnp.exp(s_ref[:, p * 2 * TILE : (p + 1) * 2 * TILE] - top)
            total = total + jnp.sum(w, axis=1, keepdims=True)
            acc = acc + jnp.dot(w.astype(jnp.bfloat16), pair(b, p, LAT), preferred_element_type=jnp.float32)
        latent = (acc / total).astype(jnp.bfloat16)
        for h in range(HEADS):
            up = jnp.dot(latent[h * TILE : (h + 1) * TILE], w_ref[h], preferred_element_type=jnp.float32)
            out_ref[h, b * TILE : (b + 1) * TILE, :] = up.astype(jnp.bfloat16)


def attention(place, vert, slash, q, kv, w):
    slots = min(12, 8 * kv.shape[2])
    smem = pl.BlockSpec(memory_space=pltpu.SMEM)
    vmem = pl.BlockSpec(memory_space=pltpu.VMEM)
    return pl.pallas_call(
        functools.partial(attend, slots),
        out_shape=jax.ShapeDtypeStruct((HEADS, ROWS, 128), jnp.bfloat16),
        in_specs=[smem, smem, smem, vmem, vmem, vmem],
        out_specs=vmem,
        scratch_shapes=[
            pltpu.SMEM((BLOCKS, 32), jnp.int32),
            pltpu.VMEM((HEADS * TILE, slots * TILE), jnp.float32),
        ],
        compiler_params=pltpu.CompilerParams(vmem_limit_bytes=40 * 1024 * 1024),
        name="attention",
    )(place, vert, slash, q, kv, w)


def device_at(zh, core, y, x, zl):
    return (((zh * 2 + core) * 4 + y) * 4 + x) * 4 + zl


def lines(swapped):
    out = []
    for zh in range(4):
        for core in range(2):
            for at in range(4):
                for zl in range(4):
                    along_x = (core == 0) != swapped
                    out.append([device_at(zh, core, *((at, n) if along_x else (n, at)), zl) for n in range(4)])
    return out


def to_all(block, groups):
    return lax.all_to_all(jnp.broadcast_to(block[None], (4, *block.shape)), ALL, 0, 0, axis_index_groups=groups)


other_core = [(device_at(a, c, 0, 0, 0) + n, device_at(a, 1 - c, 0, 0, 0) + n) for a in range(4) for c in range(2) for n in range(64)]


def on_device(queries, kv_latent, vert_tiles, slash_offsets, w_uv):
    zh, core = lax.axis_index("zh"), lax.axis_index("core")
    grp_at = (lax.axis_index("y") * 4 + lax.axis_index("x")) * 4 + lax.axis_index("zl")
    place = jnp.stack([zh * 2 + core, core]).astype(jnp.int32)
    vert, slash = vert_tiles[grp_at], slash_offsets[grp_at]
    rows = jnp.pad(kv_latent, ((0, 0), (0, WIDE - KV)))
    column = lax.all_to_all(jnp.broadcast_to(rows[None], (16, 8, WIDE)), ("zh", "zl"), 0, 0)

    def plane(depth, column):
        block = column[: 4 * depth].reshape(depth, 32, WIDE)
        block = to_all(block, lines(False))
        own = to_all(block, lines(True))
        other = lax.ppermute(own, ALL, other_core)
        kv = jnp.stack([own, other]).reshape(2, 16, depth, 32, WIDE)
        return attention(place, vert, slash, queries, kv, w_uv)

    return lax.switch(zh, [functools.partial(plane, depth) for depth in range(1, 5)], column)


def solution(mesh):
    fine = Mesh(mesh.devices.reshape(4, 2, 4, 4, 4), ALL)
    ctx, grp = ("zh", "core"), ("y", "x", "zl")
    placed = (P(grp, ctx, None), P(ctx + grp, None), P(), P(), P(grp, None, None))
    return jax.shard_map(
        on_device, mesh=fine, in_specs=placed, out_specs=P(grp, ctx, None), check_vma=False
    )
```

```python
import functools

import jax
import jax.numpy as jnp
from jax import lax
from jax.experimental import pallas as pl
from jax.experimental.pallas import tpu as pltpu
from jax.sharding import Mesh, PartitionSpec as P

TILE = 128
HEADS = 2
LAT = 512
KV = 576
WIDE = 640
ROWS = 512
BLOCKS = 4
ROW_SCALE = 192.0 ** -0.5 * 1.4426950408889634
DEAD = -1e30
STEPS = (2, 3, 4)
ALL = ("zh", "core", "y", "x", "zl")


def choose(place, vert, slash, plan_ref):
    half = place[1]
    for b in range(BLOCKS):
        i = place[0] * BLOCKS + b
        live = jnp.int32(0)
        for n in range(6):
            v = vert[n]
            live = live | jnp.where(v < i, jnp.int32(1) << v, 0)
        for n in range(4):
            v = i - slash[n]
            live = live | jnp.where(v >= 0, jnp.int32(1) << jnp.maximum(v, 0), 0)
        for n in range(12):
            plan_ref[b, n] = i
            plan_ref[BLOCKS + b, n] = i
        mine, others = jnp.int32(1), jnp.int32(0)
        for j in range(31):
            bit = (live >> j) & 1
            same = jnp.where((j >> 2) & 1 == half, bit, 0)
            plan_ref[b, mine] = jnp.where(same == 1, j, i)
            mine = mine + same
            plan_ref[BLOCKS + b, others] = jnp.where(bit - same == 1, j, i)
            others = others + bit - same
        plan_ref[b, 31] = mine
        plan_ref[BLOCKS + b, 31] = others


def choice(place, vert, slash):
    smem = pl.BlockSpec(memory_space=pltpu.SMEM)
    return pl.pallas_call(
        choose,
        out_shape=jax.ShapeDtypeStruct((2 * BLOCKS, 32), jnp.int32),
        in_specs=[smem, smem, smem],
        out_specs=smem,
        name="choice",
    )(place, vert, slash)


def steps(most):
    ends = [n for n in STEPS if n < most] + [most]
    return list(zip([0] + ends, ends))


def scored(b, under, pairs, first, plan, row, half, q_ref, kv_ref, s_ref):
    q = jnp.concatenate([q_ref[h, :, pl.ds(pl.multiple_of(b * TILE, TILE), TILE)].T for h in range(HEADS)], axis=0)

    def pair(p, width):
        pieces = []
        for n in range(2):
            tile = plan[row, 2 * p + n]
            zh, y = tile >> 3, tile & 3
            start, step = jnp.where(half == 0, 4 * y, y), jnp.where(half == 0, 1, 4)
            pieces += [kv_ref[start + step * m, zh, :, :width] for m in range(4)]
        return jnp.concatenate(pieces, axis=0)

    top = None
    for p in range(pairs):
        s = lax.dot_general(q, pair(p, KV), (((1,), (1,)), ((), ())), preferred_element_type=jnp.float32)
        s = s * ROW_SCALE
        left, right = s[:, :TILE], s[:, TILE:]
        if first and p == 0:
            at = lax.broadcasted_iota(jnp.int32, (HEADS * TILE, TILE), 0) & (TILE - 1)
            left = jnp.where(lax.broadcasted_iota(jnp.int32, (HEADS * TILE, TILE), 1) <= at, left, DEAD)
        if p >= under:
            left = left + jnp.where(2 * p < plan[row, 31], 0.0, DEAD) if p > under else left
            right = right + jnp.where(2 * p + 1 < plan[row, 31], 0.0, DEAD)
        s_ref[:, 2 * p * TILE : (2 * p + 1) * TILE] = left
        s_ref[:, (2 * p + 1) * TILE : (2 * p + 2) * TILE] = right
        t = jnp.maximum(jnp.max(left, axis=1, keepdims=True), jnp.max(right, axis=1, keepdims=True))
        top = t if top is None else jnp.maximum(top, t)
    return top, pair


def summed(pairs, pair, top, total, acc, s_ref):
    for p in range(pairs):
        w = jnp.exp2(s_ref[:, p * 2 * TILE : (p + 1) * 2 * TILE] - top)
        total = total + jnp.sum(w, axis=1, keepdims=True)
        acc = acc + jnp.dot(w.astype(jnp.bfloat16), pair(p, LAT), preferred_element_type=jnp.float32)
    return total, acc


def attend_own(most, place, plan, q_ref, kv_ref, acc_ref, top_ref, total_ref, s_ref):
    def tile(b, _):
        held = plan[b, 31]
        for under, pairs in steps(most):
            @pl.when((held > 2 * under) & (held <= 2 * pairs))
            def _(under=under, pairs=pairs):
                top, pair = scored(b, under, pairs, True, plan, b, place[1], q_ref, kv_ref, s_ref)
                total = jnp.zeros((HEADS * TILE, 1), jnp.float32)
                acc = jnp.zeros((HEADS * TILE, LAT), jnp.float32)
                total, acc = summed(pairs, pair, top, total, acc, s_ref)
                acc_ref[b] = acc
                top_ref[b] = jnp.broadcast_to(top, (HEADS * TILE, TILE))
                total_ref[b] = jnp.broadcast_to(total, (HEADS * TILE, TILE))
        return 0

    lax.fori_loop(0, BLOCKS, tile, 0)


def attend_other(most, place, plan, q_ref, kv_ref, acc_ref, top_ref, total_ref, w_ref, out_ref, s_ref):
    def tile(b, _):
        held = plan[BLOCKS + b, 31]
        for under, pairs in [(-1, 0)] + steps(most):
            @pl.when((held > 2 * under) & (held <= 2 * pairs))
            def _(under=under, pairs=pairs):
                total, acc = total_ref[b, :, :1], acc_ref[b]
                if pairs:
                    top, pair = scored(b, under, pairs, False, plan, BLOCKS + b, 1 - place[1], q_ref, kv_ref, s_ref)
                    top = jnp.maximum(top, top_ref[b, :, :1])
                    fall = jnp.exp2(top_ref[b, :, :1] - top)
                    total, acc = summed(pairs, pair, top, fall * total, fall * acc, s_ref)
                latent = (acc / total).astype(jnp.bfloat16)
                for h in range(HEADS):
                    up = jnp.dot(latent[h * TILE : (h + 1) * TILE], w_ref[h], preferred_element_type=jnp.float32)
                    out_ref[h, pl.ds(pl.multiple_of(b * TILE, TILE), TILE), :] = up.astype(jnp.bfloat16)
        return 0

    lax.fori_loop(0, BLOCKS, tile, 0)


smem = pl.BlockSpec(memory_space=pltpu.SMEM)
vmem = pl.BlockSpec(memory_space=pltpu.VMEM)


def own_half(place, plan, q, kv):
    most = min(6, 2 * kv.shape[1])
    part = jax.ShapeDtypeStruct((BLOCKS, HEADS * TILE, TILE), jnp.float32)
    return pl.pallas_call(
        functools.partial(attend_own, most),
        out_shape=(jax.ShapeDtypeStruct((BLOCKS, HEADS * TILE, LAT), jnp.float32), part, part),
        in_specs=[smem, smem, vmem, vmem],
        out_specs=(vmem, vmem, vmem),
        scratch_shapes=[pltpu.VMEM((HEADS * TILE, 2 * most * TILE), jnp.float32)],
        compiler_params=pltpu.CompilerParams(vmem_limit_bytes=16 * 1024 * 1024),
        cost_estimate=pl.CostEstimate(flops=1 << 31, bytes_accessed=1 << 22, transcendentals=1 << 20),
        name="own_half",
    )(place, plan, q, kv)


def other_half(place, plan, q, kv, parts, w):
    most = min(6, 2 * kv.shape[1])
    return pl.pallas_call(
        functools.partial(attend_other, most),
        out_shape=jax.ShapeDtypeStruct((HEADS, ROWS, 128), jnp.bfloat16),
        in_specs=[smem, smem, vmem, vmem, vmem, vmem, vmem, vmem],
        out_specs=vmem,
        scratch_shapes=[pltpu.VMEM((HEADS * TILE, 2 * most * TILE), jnp.float32)],
        compiler_params=pltpu.CompilerParams(vmem_limit_bytes=16 * 1024 * 1024),
        cost_estimate=pl.CostEstimate(flops=1 << 31, bytes_accessed=1 << 22, transcendentals=1 << 20),
        name="other_half",
    )(place, plan, q, kv, *parts, w)


def device_at(zh, core, y, x, zl):
    return (((zh * 2 + core) * 4 + y) * 4 + x) * 4 + zl


def lines(swapped):
    out = []
    for zh in range(4):
        for core in range(2):
            for at in range(4):
                for zl in range(4):
                    along_x = (core == 0) != swapped
                    out.append([device_at(zh, core, *((at, n) if along_x else (n, at)), zl) for n in range(4)])
    return out


def to_all(block, groups):
    return lax.all_to_all(jnp.broadcast_to(block[None], (4, *block.shape)), ALL, 0, 0, axis_index_groups=groups)


other_core = [(device_at(a, c, 0, 0, 0) + n, device_at(a, 1 - c, 0, 0, 0) + n) for a in range(4) for c in range(2) for n in range(64)]


def on_device(queries, kv_latent, vert_tiles, slash_offsets, w_uv):
    zh, core = lax.axis_index("zh"), lax.axis_index("core")
    grp_at = (lax.axis_index("y") * 4 + lax.axis_index("x")) * 4 + lax.axis_index("zl")
    place = jnp.stack([zh * 2 + core, core]).astype(jnp.int32)
    rows = jnp.pad(kv_latent, ((0, 0), (0, WIDE - KV)))
    column = lax.all_to_all(jnp.broadcast_to(rows[None], (16, 8, WIDE)), ("zh", "zl"), 0, 0)

    plan = choice(place, vert_tiles[grp_at], slash_offsets[grp_at])
    turned = queries.transpose(0, 2, 1)

    def plane(depth, column):
        block = column[: 4 * depth].reshape(depth, 32, WIDE)
        block = to_all(block, lines(False))
        own = to_all(block, lines(True)).reshape(16, depth, 32, WIDE)
        other = lax.ppermute(own, ALL, other_core)
        parts = own_half(place, plan, turned, own)
        return other_half(place, plan, turned, other, parts, w_uv)

    return lax.switch(zh, [functools.partial(plane, depth) for depth in range(1, 5)], column)


def solution(mesh):
    fine = Mesh(mesh.devices.reshape(4, 2, 4, 4, 4), ALL)
    ctx, grp = ("zh", "core"), ("y", "x", "zl")
    placed = (P(grp, ctx, None), P(ctx + grp, None), P(), P(), P(grp, None, None))
    return jax.shard_map(
        on_device, mesh=fine, in_specs=placed, out_specs=P(grp, ctx, None), check_vma=False
    )
```

```python
import functools

import jax
import jax.numpy as jnp
from jax import lax
from jax.experimental import pallas as pl
from jax.experimental.pallas import tpu as pltpu
from jax.sharding import Mesh, PartitionSpec as P

TILE = 128
HEADS = 2
LAT = 512
KV = 576
ROWS = 512
BLOCKS = 4
ROW_SCALE = 192.0 ** -0.5 * 1.4426950408889634
DEAD = -1e30
OWN_PAIRS = 4
OTHER_PAIRS = 4
ALL = ("zh", "core", "y", "x", "zl")


def choose(place, vert, slash, plan_ref):
    half = place[1]
    for b in range(BLOCKS):
        i = place[0] * BLOCKS + b
        live = jnp.int32(0)
        for n in range(6):
            v = vert[n]
            live = live | jnp.where(v < i, jnp.int32(1) << v, 0)
        for n in range(4):
            v = i - slash[n]
            live = live | jnp.where(v >= 0, jnp.int32(1) << jnp.maximum(v, 0), 0)
        for n in range(12):
            plan_ref[b, n] = i
            plan_ref[BLOCKS + b, n] = i
        mine, others = jnp.int32(1), jnp.int32(0)
        for j in range(31):
            bit = (live >> j) & 1
            same = jnp.where((j >> 2) & 1 == half, bit, 0)
            plan_ref[b, mine] = jnp.where(same == 1, j, i)
            mine = mine + same
            plan_ref[BLOCKS + b, others] = jnp.where(bit - same == 1, j, i)
            others = others + bit - same
        plan_ref[b, 31] = mine
        plan_ref[BLOCKS + b, 31] = others


def choice(place, vert, slash):
    smem = pl.BlockSpec(memory_space=pltpu.SMEM)
    return pl.pallas_call(
        choose,
        out_shape=jax.ShapeDtypeStruct((2 * BLOCKS, 32), jnp.int32),
        in_specs=[smem, smem, smem],
        out_specs=smem,
        name="choice",
    )(place, vert, slash)


def pair_of(p, plan, row, half, kv_ref, rotary):
    lane = lax.broadcasted_iota(jnp.int32, (16, TILE), 1)
    sides = [(lane < 64).astype(jnp.bfloat16), (lane >= 64).astype(jnp.bfloat16)]
    pieces = []
    for n in range(2):
        tile = plan[row, 2 * p + n]
        zh, y = tile >> 3, tile & 3
        start, step = jnp.where(half == 0, 4 * y, y), jnp.where(half == 0, 1, 4)
        for m in range(4):
            at = start + step * m
            parts = [kv_ref[at, zh, 32 * t : 32 * t + 32, :] for t in range(4)]
            if rotary:
                both = kv_ref[at, zh, 128:, :]
                parts.append(jnp.concatenate([both * side for side in sides], axis=0))
            pieces.append(jnp.concatenate(parts, axis=1))
    return jnp.concatenate(pieces, axis=0)


def scores(q, p, own_tile, plan, row, half, kv_ref):
    s = lax.dot_general(
        q, pair_of(p, plan, row, half, kv_ref, True), (((1,), (1,)), ((), ())), preferred_element_type=jnp.float32
    )
    s = s * ROW_SCALE
    left, right = s[:, :TILE], s[:, TILE:]
    if own_tile:
        at = lax.broadcasted_iota(jnp.int32, (HEADS * TILE, TILE), 0) & (TILE - 1)
        left = jnp.where(lax.broadcasted_iota(jnp.int32, (HEADS * TILE, TILE), 1) <= at, left, DEAD)
    else:
        left = left + jnp.where(2 * p < plan[row, 31], 0.0, DEAD)
    right = right + jnp.where(2 * p + 1 < plan[row, 31], 0.0, DEAD)
    return jnp.concatenate([left, right], axis=1)


def wide(column, times):
    return jnp.concatenate([column] * times, axis=1)


def every_lane(column):
    return jnp.broadcast_to(column, (HEADS * TILE, TILE))


def weighted(s, top, p, plan, row, half, kv_ref):
    w = jnp.exp2(s - wide(top, 2))
    values = pair_of(p, plan, row, half, kv_ref, False)
    return w[:, :TILE] + w[:, TILE:], jnp.dot(w.astype(jnp.bfloat16), values, preferred_element_type=jnp.float32)


def many(q, pairs, own, plan, row, half, kv_ref, s_ref, top, total, acc):
    start, largest = top, None
    for p in range(pairs):
        s = scores(q, p, own and p == 0, plan, row, half, kv_ref)
        s_ref[:, p * 2 * TILE : (p + 1) * 2 * TILE] = s
        t = jnp.max(s, axis=1, keepdims=True)
        largest = t if largest is None else jnp.maximum(largest, t)
    top = every_lane(largest)
    if start is not None:
        top = jnp.maximum(start, top)
        fall = jnp.exp2(start - top)
        total, acc = fall * total, wide(fall, LAT // TILE) * acc
    add = None
    for p in range(pairs):
        t, a = weighted(s_ref[:, p * 2 * TILE : (p + 1) * 2 * TILE], top, p, plan, row, half, kv_ref)
        add, acc = (t if add is None else add + t), (a if acc is None else acc + a)
    add = every_lane(jnp.sum(add, axis=1, keepdims=True))
    return top, add if total is None else total + add, acc


def rest(pairs, plan, first_row, half, kv_ref, q_ref, acc_ref, top_ref, total_ref):
    def tile(b, _):
        row = first_row + b

        def one(p, _):
            s = scores(q_ref[b], p, False, plan, row, half, kv_ref)
            top = jnp.maximum(every_lane(jnp.max(s, axis=1, keepdims=True)), top_ref[b])
            fall = jnp.exp2(top_ref[b] - top)
            t, a = weighted(s, top, p, plan, row, half, kv_ref)
            acc_ref[b] = wide(fall, LAT // TILE) * acc_ref[b] + a
            total_ref[b] = fall * total_ref[b] + every_lane(jnp.sum(t, axis=1, keepdims=True))
            top_ref[b] = top
            return 0

        return lax.fori_loop(pairs, (plan[row, 31] + 1) >> 1, one, 0)

    lax.fori_loop(0, BLOCKS, tile, 0)


def attend_own(pairs, more, place, plan, turned_ref, kv_ref, q_ref, acc_ref, top_ref, total_ref, s_ref):
    for b in range(BLOCKS):
        turned = [turned_ref[h, :, b * TILE : (b + 1) * TILE] for h in range(HEADS)]
        q = jnp.concatenate([jnp.concatenate([t, t[LAT:]], axis=0).T for t in turned], axis=0)
        q_ref[b] = q
        top, total, acc = many(q, pairs, True, plan, b, place[1], kv_ref, s_ref.at[b % 2], None, None, None)
        acc_ref[b] = acc
        top_ref[b] = top
        total_ref[b] = total
    if more:
        rest(pairs, plan, 0, place[1], kv_ref, q_ref, acc_ref, top_ref, total_ref)


def attend_other(pairs, more, place, plan, kv_ref, q_ref, acc_in, top_in, total_in, w_ref, out_ref, s_ref, latent_ref, *state):
    half = 1 - place[1]
    if more:
        for held, given in zip(state, (acc_in, top_in, total_in)):
            held[...] = given[...]
        rest(pairs, plan, BLOCKS, half, kv_ref, q_ref, *state)
    acc_ref, top_ref, total_ref = state or (acc_in, top_in, total_in)
    for b in range(BLOCKS):
        top, total, acc = many(
            q_ref[b], pairs, False, plan, BLOCKS + b, half, kv_ref, s_ref.at[b % 2], top_ref[b], total_ref[b], acc_ref[b]
        )
        latent_ref[b] = (acc * wide(1.0 / total, LAT // TILE)).astype(jnp.bfloat16)
    for h in range(HEADS):
        latent = jnp.concatenate([latent_ref[b, h * TILE : (h + 1) * TILE] for b in range(BLOCKS)], axis=0)
        up = jnp.dot(latent, w_ref[h], preferred_element_type=jnp.float32)
        out_ref[h] = up.astype(jnp.bfloat16)


smem = pl.BlockSpec(memory_space=pltpu.SMEM)
vmem = pl.BlockSpec(memory_space=pltpu.VMEM)


def pack(depth, column_ref, block_ref):
    for zh in range(depth):
        rows = jnp.concatenate([column_ref[4 * zh + n].astype(jnp.float32) for n in range(4)], axis=0)
        rotary = jnp.concatenate([rows[:16, LAT:], rows[16:, LAT:]], axis=1)
        block = jnp.concatenate([rows[:, n * TILE : (n + 1) * TILE] for n in range(4)] + [rotary], axis=0)
        block = block.astype(jnp.bfloat16)
        for to in range(4):
            block_ref[to, zh] = block


def packed(depth, column):
    return pl.pallas_call(
        functools.partial(pack, depth),
        out_shape=jax.ShapeDtypeStruct((4, depth, 144, TILE), jnp.bfloat16),
        in_specs=[vmem],
        out_specs=vmem,
        name="packed",
    )(column)


part = jax.ShapeDtypeStruct((BLOCKS, HEADS * TILE, TILE), jnp.float32)
accumulated = (jax.ShapeDtypeStruct((BLOCKS, HEADS * TILE, LAT), jnp.float32), part, part)


def own_half(place, plan, q, kv):
    most = min(6, 2 * kv.shape[1])
    pairs = min(OWN_PAIRS, most)
    return pl.pallas_call(
        functools.partial(attend_own, pairs, most > pairs),
        out_shape=(jax.ShapeDtypeStruct((BLOCKS, HEADS * TILE, LAT + TILE), jnp.bfloat16), *accumulated),
        in_specs=[smem, smem, vmem, vmem],
        out_specs=(vmem, vmem, vmem, vmem),
        scratch_shapes=[pltpu.VMEM((2, HEADS * TILE, 2 * pairs * TILE), jnp.float32)],
        compiler_params=pltpu.CompilerParams(vmem_limit_bytes=16 * 1024 * 1024),
        cost_estimate=pl.CostEstimate(flops=1 << 31, bytes_accessed=1 << 22, transcendentals=1 << 20),
        name="own_half",
    )(place, plan, q, kv)


def other_half(place, plan, kv, parts, w):
    most = min(6, 2 * kv.shape[1])
    pairs = min(OTHER_PAIRS, most)
    return pl.pallas_call(
        functools.partial(attend_other, pairs, most > pairs),
        out_shape=jax.ShapeDtypeStruct((HEADS, ROWS, 128), jnp.bfloat16),
        in_specs=[smem, smem, vmem, vmem, vmem, vmem, vmem, vmem],
        out_specs=vmem,
        scratch_shapes=[
            pltpu.VMEM((2, HEADS * TILE, 2 * pairs * TILE), jnp.float32),
            pltpu.VMEM((BLOCKS, HEADS * TILE, LAT), jnp.bfloat16),
            *(pltpu.VMEM(a.shape, a.dtype) for a in accumulated if most > pairs),
        ],
        compiler_params=pltpu.CompilerParams(vmem_limit_bytes=16 * 1024 * 1024),
        cost_estimate=pl.CostEstimate(flops=1 << 31, bytes_accessed=1 << 22, transcendentals=1 << 20),
        name="other_half",
    )(place, plan, kv, *parts, w)


def device_at(zh, core, y, x, zl):
    return (((zh * 2 + core) * 4 + y) * 4 + x) * 4 + zl


def lines(swapped):
    out = []
    for zh in range(4):
        for core in range(2):
            for at in range(4):
                for zl in range(4):
                    along_x = (core == 0) != swapped
                    out.append([device_at(zh, core, *((at, n) if along_x else (n, at)), zl) for n in range(4)])
    return out


def to_all(blocks, groups):
    return lax.all_to_all(blocks, ALL, 0, 0, axis_index_groups=groups)


other_core = [(device_at(a, c, 0, 0, 0) + n, device_at(a, 1 - c, 0, 0, 0) + n) for a in range(4) for c in range(2) for n in range(64)]


def on_device(queries, kv_latent, vert_tiles, slash_offsets, w_uv):
    zh, core = lax.axis_index("zh"), lax.axis_index("core")
    grp_at = (lax.axis_index("y") * 4 + lax.axis_index("x")) * 4 + lax.axis_index("zl")
    place = jnp.stack([zh * 2 + core, core]).astype(jnp.int32)
    column = lax.all_to_all(jnp.broadcast_to(kv_latent[None], (16, 8, KV)), ("zh", "zl"), 0, 0)
    plan = choice(place, vert_tiles[grp_at], slash_offsets[grp_at])
    turned = queries.transpose(0, 2, 1)

    def plane(depth, column):
        block = to_all(packed(depth, column), lines(False))
        own = to_all(jnp.broadcast_to(block[None], (4, *block.shape)), lines(True)).reshape(16, depth, 144, TILE)
        other = lax.ppermute(own, ALL, other_core)
        parts = own_half(place, plan, turned, own)
        return other_half(place, plan, other, parts, w_uv)

    return lax.switch(zh, [functools.partial(plane, depth) for depth in range(1, 5)], column)


def solution(mesh):
    fine = Mesh(mesh.devices.reshape(4, 2, 4, 4, 4), ALL)
    ctx, grp = ("zh", "core"), ("y", "x", "zl")
    placed = (P(grp, ctx, None), P(ctx + grp, None), P(), P(), P(grp, None, None))
    return jax.shard_map(
        on_device, mesh=fine, in_specs=placed, out_specs=P(grp, ctx, None), check_vma=False
    )
```

```python
import functools

import jax
import jax.numpy as jnp
from jax import lax
from jax.experimental import pallas as pl
from jax.experimental.pallas import tpu as pltpu
from jax.sharding import Mesh, PartitionSpec as P

TILE = 128
HEADS = 2
LAT = 512
KV = 576
ROWS = 512
BLOCKS = 4
ROW_SCALE = 192.0 ** -0.5 * 1.4426950408889634
DEAD = -1e30
OWN_PAIRS = 4
OTHER_PAIRS = 4
ALL = ("zh", "core", "y", "x", "zl")


def choose(place, vert, slash, plan_ref):
    half = place[1]
    for b in range(BLOCKS):
        i = place[0] * BLOCKS + b
        live = jnp.int32(0)
        for n in range(6):
            v = vert[n]
            live = live | jnp.where(v < i, jnp.int32(1) << v, 0)
        for n in range(4):
            v = i - slash[n]
            live = live | jnp.where(v >= 0, jnp.int32(1) << jnp.maximum(v, 0), 0)
        for n in range(12):
            plan_ref[b, n] = i
            plan_ref[BLOCKS + b, n] = i
        mine, others = jnp.int32(1), jnp.int32(0)
        for j in range(31):
            bit = (live >> j) & 1
            same = jnp.where((j >> 2) & 1 == half, bit, 0)
            plan_ref[b, mine] = jnp.where(same == 1, j, i)
            mine = mine + same
            plan_ref[BLOCKS + b, others] = jnp.where(bit - same == 1, j, i)
            others = others + bit - same
        plan_ref[b, 31] = mine
        plan_ref[BLOCKS + b, 31] = others


def choice(place, vert, slash):
    smem = pl.BlockSpec(memory_space=pltpu.SMEM)
    return pl.pallas_call(
        choose,
        out_shape=jax.ShapeDtypeStruct((2 * BLOCKS, 32), jnp.int32),
        in_specs=[smem, smem, smem],
        out_specs=smem,
        name="choice",
    )(place, vert, slash)


def pair_of(p, plan, row, half, kv_ref, rotary):
    lane = lax.broadcasted_iota(jnp.int32, (16, TILE), 1)
    sides = [(lane < 64).astype(jnp.bfloat16), (lane >= 64).astype(jnp.bfloat16)]
    pieces = []
    for n in range(2):
        tile = plan[row, 2 * p + n]
        zh, y = tile >> 3, tile & 3
        start, step = jnp.where(half == 0, 4 * y, y), jnp.where(half == 0, 1, 4)
        for m in range(4):
            at = start + step * m
            for side in range(2):
                parts = [kv_ref[at, zh, 64 * side + 16 * t : 64 * side + 16 * t + 16, :] for t in range(4)]
                if rotary:
                    parts.append(kv_ref[at, zh, 128:, :] * sides[side])
                pieces.append(jnp.concatenate(parts, axis=1))
    return jnp.concatenate(pieces, axis=0)


def scores(q, p, own_tile, plan, row, half, kv_ref):
    s = lax.dot_general(
        q, pair_of(p, plan, row, half, kv_ref, True), (((1,), (1,)), ((), ())), preferred_element_type=jnp.float32
    )
    s = s * ROW_SCALE
    left, right = s[:, :TILE], s[:, TILE:]
    if own_tile:
        at = lax.broadcasted_iota(jnp.int32, (HEADS * TILE, TILE), 0) & (TILE - 1)
        col = lax.broadcasted_iota(jnp.int32, (HEADS * TILE, TILE), 1)
        col = (col & 99) | ((col & 12) << 1) | ((col & 16) >> 2)
        left = jnp.where(col <= at, left, DEAD)
    else:
        left = left + jnp.where(2 * p < plan[row, 31], 0.0, DEAD)
    right = right + jnp.where(2 * p + 1 < plan[row, 31], 0.0, DEAD)
    return jnp.concatenate([left, right], axis=1)


def wide(column, times):
    return jnp.concatenate([column] * times, axis=1)


def every_lane(column):
    return jnp.broadcast_to(column, (HEADS * TILE, TILE))


def weighted(s, top, p, plan, row, half, kv_ref):
    w = jnp.exp2(s - wide(top, 2))
    values = pair_of(p, plan, row, half, kv_ref, False)
    return w[:, :TILE] + w[:, TILE:], jnp.dot(w.astype(jnp.bfloat16), values, preferred_element_type=jnp.float32)


def many(q, pairs, own, plan, row, half, kv_ref, s_ref, top, total, acc):
    start, largest = top, None
    for p in range(pairs):
        s = scores(q, p, own and p == 0, plan, row, half, kv_ref)
        s_ref[:, p * 2 * TILE : (p + 1) * 2 * TILE] = s
        t = jnp.max(s, axis=1, keepdims=True)
        largest = t if largest is None else jnp.maximum(largest, t)
    top = every_lane(largest)
    if start is not None:
        top = jnp.maximum(start, top)
        fall = jnp.exp2(start - top)
        total, acc = fall * total, wide(fall, LAT // TILE) * acc
    add = None
    for p in range(pairs):
        t, a = weighted(s_ref[:, p * 2 * TILE : (p + 1) * 2 * TILE], top, p, plan, row, half, kv_ref)
        add, acc = (t if add is None else add + t), (a if acc is None else acc + a)
    add = every_lane(jnp.sum(add, axis=1, keepdims=True))
    return top, add if total is None else total + add, acc


def rest(pairs, plan, first_row, half, kv_ref, q_ref, acc_ref, top_ref, total_ref):
    def tile(b, _):
        row = first_row + b

        def one(p, _):
            s = scores(q_ref[b], p, False, plan, row, half, kv_ref)
            top = jnp.maximum(every_lane(jnp.max(s, axis=1, keepdims=True)), top_ref[b])
            fall = jnp.exp2(top_ref[b] - top)
            t, a = weighted(s, top, p, plan, row, half, kv_ref)
            acc_ref[b] = wide(fall, LAT // TILE) * acc_ref[b] + a
            total_ref[b] = fall * total_ref[b] + every_lane(jnp.sum(t, axis=1, keepdims=True))
            top_ref[b] = top
            return 0

        return lax.fori_loop(pairs, (plan[row, 31] + 1) >> 1, one, 0)

    lax.fori_loop(0, BLOCKS, tile, 0)


def attend_own(pairs, more, place, plan, turned_ref, kv_ref, q_ref, acc_ref, top_ref, total_ref, s_ref):
    for b in range(BLOCKS):
        turned = [turned_ref[h, :, b * TILE : (b + 1) * TILE] for h in range(HEADS)]
        q = jnp.concatenate([jnp.concatenate([t, t[LAT:]], axis=0).T for t in turned], axis=0)
        q_ref[b] = q
        top, total, acc = many(q, pairs, True, plan, b, place[1], kv_ref, s_ref.at[b % 2], None, None, None)
        acc_ref[b] = acc
        top_ref[b] = top
        total_ref[b] = total
    if more:
        rest(pairs, plan, 0, place[1], kv_ref, q_ref, acc_ref, top_ref, total_ref)


def attend_other(pairs, more, place, plan, kv_ref, q_ref, acc_in, top_in, total_in, w_ref, out_ref, s_ref, latent_ref, *state):
    half = 1 - place[1]
    if more:
        for held, given in zip(state, (acc_in, top_in, total_in)):
            held[...] = given[...]
        rest(pairs, plan, BLOCKS, half, kv_ref, q_ref, *state)
    acc_ref, top_ref, total_ref = state or (acc_in, top_in, total_in)
    for b in range(BLOCKS):
        top, total, acc = many(
            q_ref[b], pairs, False, plan, BLOCKS + b, half, kv_ref, s_ref.at[b % 2], top_ref[b], total_ref[b], acc_ref[b]
        )
        latent_ref[b] = (acc * wide(1.0 / total, LAT // TILE)).astype(jnp.bfloat16)
    for h in range(HEADS):
        latent = jnp.concatenate([latent_ref[b, h * TILE : (h + 1) * TILE] for b in range(BLOCKS)], axis=0)
        up = jnp.dot(latent, w_ref[h], preferred_element_type=jnp.float32)
        out_ref[h] = up.astype(jnp.bfloat16)


smem = pl.BlockSpec(memory_space=pltpu.SMEM)
vmem = pl.BlockSpec(memory_space=pltpu.VMEM)


def lay_beside(rows_ref, out_ref):
    rows = rows_ref[...].astype(jnp.float32)
    low, high = rows[:4], rows[4:]
    block = jnp.concatenate([low[:, :LAT], high[:, :LAT], low[:, LAT:], high[:, LAT:]], axis=1).astype(jnp.bfloat16)
    for n in range(16):
        out_ref[n] = block


def beside(rows):
    return pl.pallas_call(
        lay_beside,
        out_shape=jax.ShapeDtypeStruct((16, 4, 2 * KV), jnp.bfloat16),
        in_specs=[vmem],
        out_specs=vmem,
        name="beside",
    )(rows)


def pack(depth, column_ref, block_ref):
    for zh in range(depth):
        rows = jnp.concatenate([column_ref[4 * zh + n].astype(jnp.float32) for n in range(4)], axis=0)
        block = jnp.concatenate([rows[:, n * TILE : (n + 1) * TILE] for n in range(9)], axis=0).astype(jnp.bfloat16)
        for to in range(4):
            block_ref[to, zh] = block


def packed(depth, column):
    return pl.pallas_call(
        functools.partial(pack, depth),
        out_shape=jax.ShapeDtypeStruct((4, depth, 144, TILE), jnp.bfloat16),
        in_specs=[vmem],
        out_specs=vmem,
        name="packed",
    )(column)


part = jax.ShapeDtypeStruct((BLOCKS, HEADS * TILE, TILE), jnp.float32)
accumulated = (jax.ShapeDtypeStruct((BLOCKS, HEADS * TILE, LAT), jnp.float32), part, part)


def own_half(place, plan, q, kv):
    most = min(6, 2 * kv.shape[1])
    pairs = min(OWN_PAIRS, most)
    return pl.pallas_call(
        functools.partial(attend_own, pairs, most > pairs),
        out_shape=(jax.ShapeDtypeStruct((BLOCKS, HEADS * TILE, LAT + TILE), jnp.bfloat16), *accumulated),
        in_specs=[smem, smem, vmem, vmem],
        out_specs=(vmem, vmem, vmem, vmem),
        scratch_shapes=[pltpu.VMEM((2, HEADS * TILE, 2 * pairs * TILE), jnp.float32)],
        compiler_params=pltpu.CompilerParams(vmem_limit_bytes=16 * 1024 * 1024),
        cost_estimate=pl.CostEstimate(flops=1 << 31, bytes_accessed=1 << 22, transcendentals=1 << 20),
        name="own_half",
    )(place, plan, q, kv)


def other_half(place, plan, kv, parts, w):
    most = min(6, 2 * kv.shape[1])
    pairs = min(OTHER_PAIRS, most)
    return pl.pallas_call(
        functools.partial(attend_other, pairs, most > pairs),
        out_shape=jax.ShapeDtypeStruct((HEADS, ROWS, 128), jnp.bfloat16),
        in_specs=[smem, smem, vmem, vmem, vmem, vmem, vmem, vmem],
        out_specs=vmem,
        scratch_shapes=[
            pltpu.VMEM((2, HEADS * TILE, 2 * pairs * TILE), jnp.float32),
            pltpu.VMEM((BLOCKS, HEADS * TILE, LAT), jnp.bfloat16),
            *(pltpu.VMEM(a.shape, a.dtype) for a in accumulated if most > pairs),
        ],
        compiler_params=pltpu.CompilerParams(vmem_limit_bytes=16 * 1024 * 1024),
        cost_estimate=pl.CostEstimate(flops=1 << 31, bytes_accessed=1 << 22, transcendentals=1 << 20),
        name="other_half",
    )(place, plan, kv, *parts, w)


def device_at(zh, core, y, x, zl):
    return (((zh * 2 + core) * 4 + y) * 4 + x) * 4 + zl


def lines(swapped):
    out = []
    for zh in range(4):
        for core in range(2):
            for at in range(4):
                for zl in range(4):
                    along_x = (core == 0) != swapped
                    out.append([device_at(zh, core, *((at, n) if along_x else (n, at)), zl) for n in range(4)])
    return out


def to_all(blocks, groups):
    return lax.all_to_all(blocks, ALL, 0, 0, axis_index_groups=groups)


other_core = [(device_at(a, c, 0, 0, 0) + n, device_at(a, 1 - c, 0, 0, 0) + n) for a in range(4) for c in range(2) for n in range(64)]


def on_device(queries, kv_latent, vert_tiles, slash_offsets, w_uv):
    zh, core = lax.axis_index("zh"), lax.axis_index("core")
    grp_at = (lax.axis_index("y") * 4 + lax.axis_index("x")) * 4 + lax.axis_index("zl")
    place = jnp.stack([zh * 2 + core, core]).astype(jnp.int32)
    column = lax.all_to_all(beside(kv_latent), ("zh", "zl"), 0, 0)
    plan = choice(place, vert_tiles[grp_at], slash_offsets[grp_at])
    turned = queries.transpose(0, 2, 1)

    def plane(depth, column):
        block = to_all(packed(depth, column), lines(False))
        own = to_all(jnp.broadcast_to(block[None], (4, *block.shape)), lines(True)).reshape(16, depth, 144, TILE)
        other = lax.ppermute(own, ALL, other_core)
        parts = own_half(place, plan, turned, own)
        return other_half(place, plan, other, parts, w_uv)

    return lax.switch(zh, [functools.partial(plane, depth) for depth in range(1, 5)], column)


def solution(mesh):
    fine = Mesh(mesh.devices.reshape(4, 2, 4, 4, 4), ALL)
    ctx, grp = ("zh", "core"), ("y", "x", "zl")
    placed = (P(grp, ctx, None), P(ctx + grp, None), P(), P(), P(grp, None, None))
    return jax.shard_map(
        on_device, mesh=fine, in_specs=placed, out_specs=P(grp, ctx, None), check_vma=False
    )
```

```python
import functools

import jax
import jax.numpy as jnp
from jax import lax
from jax.experimental import pallas as pl
from jax.experimental.pallas import tpu as pltpu
from jax.sharding import Mesh, PartitionSpec as P

TILE = 128
HEADS = 2
LAT = 512
KV = 576
ROWS = 512
BLOCKS = 4
ROW_SCALE = 192.0 ** -0.5 * 1.4426950408889634
DEAD = -1e30
OWN_PAIRS = 4
OTHER_PAIRS = 4
ALL = ("zh", "core", "y", "x", "zl")


def choose(place, vert, slash, plan_ref):
    half = place[1]
    for b in range(BLOCKS):
        i = place[0] * BLOCKS + b
        live = jnp.int32(0)
        for n in range(6):
            v = vert[n]
            live = live | jnp.where(v < i, jnp.int32(1) << v, 0)
        for n in range(4):
            v = i - slash[n]
            live = live | jnp.where(v >= 0, jnp.int32(1) << jnp.maximum(v, 0), 0)
        for n in range(12):
            plan_ref[b, n] = i
            plan_ref[BLOCKS + b, n] = i
        mine, others = jnp.int32(1), jnp.int32(0)
        for j in range(31):
            bit = (live >> j) & 1
            same = jnp.where((j >> 2) & 1 == half, bit, 0)
            plan_ref[b, mine] = jnp.where(same == 1, j, i)
            mine = mine + same
            plan_ref[BLOCKS + b, others] = jnp.where(bit - same == 1, j, i)
            others = others + bit - same
        plan_ref[b, 31] = mine
        plan_ref[BLOCKS + b, 31] = others


def choice(place, vert, slash):
    smem = pl.BlockSpec(memory_space=pltpu.SMEM)
    return pl.pallas_call(
        choose,
        out_shape=jax.ShapeDtypeStruct((2 * BLOCKS, 32), jnp.int32),
        in_specs=[smem, smem, smem],
        out_specs=smem,
        name="choice",
    )(place, vert, slash)


def pair_of(p, plan, row, half, kv_ref, rotary):
    lane = lax.broadcasted_iota(jnp.int32, (16, TILE), 1)
    sides = [(lane < 64).astype(jnp.bfloat16), (lane >= 64).astype(jnp.bfloat16)]
    pieces = []
    for n in range(2):
        tile = plan[row, 2 * p + n]
        zh, y = tile >> 3, tile & 3
        start, step = jnp.where(half == 0, 4 * y, y), jnp.where(half == 0, 1, 4)
        for m in range(4):
            at = start + step * m
            for side in range(2):
                parts = [kv_ref[at, zh, 64 * side + 16 * t : 64 * side + 16 * t + 16, :] for t in range(4)]
                if rotary:
                    parts.append(kv_ref[at, zh, 128:, :] * sides[side])
                pieces.append(jnp.concatenate(parts, axis=1))
    return jnp.concatenate(pieces, axis=0)


def scores(q, p, own_tile, plan, row, half, kv_ref):
    s = lax.dot_general(
        q, pair_of(p, plan, row, half, kv_ref, True), (((1,), (1,)), ((), ())), preferred_element_type=jnp.float32
    )
    s = s * ROW_SCALE
    left, right = s[:, :TILE], s[:, TILE:]
    if own_tile:
        at = lax.broadcasted_iota(jnp.int32, (HEADS * TILE, TILE), 0) & (TILE - 1)
        col = lax.broadcasted_iota(jnp.int32, (HEADS * TILE, TILE), 1)
        col = (col & 99) | ((col & 12) << 1) | ((col & 16) >> 2)
        left = jnp.where(col <= at, left, DEAD)
    else:
        left = left + jnp.where(2 * p < plan[row, 31], 0.0, DEAD)
    right = right + jnp.where(2 * p + 1 < plan[row, 31], 0.0, DEAD)
    return jnp.concatenate([left, right], axis=1)


def wide(column, times):
    return jnp.concatenate([column] * times, axis=1)


def every_lane(column):
    return jnp.broadcast_to(column, (HEADS * TILE, TILE))


def weighted(s, top, p, plan, row, half, kv_ref):
    w = jnp.exp2(s - wide(top, 2))
    values = pair_of(p, plan, row, half, kv_ref, False)
    return w[:, :TILE] + w[:, TILE:], jnp.dot(w.astype(jnp.bfloat16), values, preferred_element_type=jnp.float32)


def many(q, pairs, own, plan, row, half, kv_ref, s_ref, top, total, acc):
    start, largest = top, None
    for p in range(pairs):
        s = scores(q, p, own and p == 0, plan, row, half, kv_ref)
        s_ref[:, p * 2 * TILE : (p + 1) * 2 * TILE] = s
        t = jnp.max(s, axis=1, keepdims=True)
        largest = t if largest is None else jnp.maximum(largest, t)
    top = every_lane(largest)
    if start is not None:
        top = jnp.maximum(start, top)
        fall = jnp.exp2(start - top)
        total, acc = fall * total, wide(fall, LAT // TILE) * acc
    add = None
    for p in range(pairs):
        t, a = weighted(s_ref[:, p * 2 * TILE : (p + 1) * 2 * TILE], top, p, plan, row, half, kv_ref)
        add, acc = (t if add is None else add + t), (a if acc is None else acc + a)
    add = every_lane(jnp.sum(add, axis=1, keepdims=True))
    return top, add if total is None else total + add, acc


def rest(pairs, plan, first_row, half, kv_ref, q_ref, acc_ref, top_ref, total_ref):
    def tile(b, _):
        row = first_row + b

        def one(p, _):
            s = scores(q_ref[b], p, False, plan, row, half, kv_ref)
            top = jnp.maximum(every_lane(jnp.max(s, axis=1, keepdims=True)), top_ref[b])
            fall = jnp.exp2(top_ref[b] - top)
            t, a = weighted(s, top, p, plan, row, half, kv_ref)
            acc_ref[b] = wide(fall, LAT // TILE) * acc_ref[b] + a
            total_ref[b] = fall * total_ref[b] + every_lane(jnp.sum(t, axis=1, keepdims=True))
            top_ref[b] = top
            return 0

        return lax.fori_loop(pairs, (plan[row, 31] + 1) >> 1, one, 0)

    lax.fori_loop(0, BLOCKS, tile, 0)


def attend_own(pairs, more, place, plan, turned_ref, kv_ref, q_ref, acc_ref, top_ref, total_ref, s_ref):
    for b in range(BLOCKS):
        turned = [turned_ref[h, :, b * TILE : (b + 1) * TILE] for h in range(HEADS)]
        q = jnp.concatenate([jnp.concatenate([t, t[LAT:]], axis=0).T for t in turned], axis=0)
        q_ref[b] = q
        top, total, acc = many(q, pairs, True, plan, b, place[1], kv_ref, s_ref.at[b % 2], None, None, None)
        acc_ref[b] = acc
        top_ref[b] = top
        total_ref[b] = total
    if more:
        rest(pairs, plan, 0, place[1], kv_ref, q_ref, acc_ref, top_ref, total_ref)


def attend_other(pairs, more, place, plan, kv_ref, q_ref, acc_in, top_in, total_in, w_ref, out_ref, s_ref, *state):
    half = 1 - place[1]
    if more:
        for held, given in zip(state, (acc_in, top_in, total_in)):
            held[...] = given[...]
        rest(pairs, plan, BLOCKS, half, kv_ref, q_ref, *state)
    acc_ref, top_ref, total_ref = state or (acc_in, top_in, total_in)
    for b in range(BLOCKS):
        top, total, acc = many(
            q_ref[b], pairs, False, plan, BLOCKS + b, half, kv_ref, s_ref.at[b % 2], top_ref[b], total_ref[b], acc_ref[b]
        )
        latent = (acc * wide(1.0 / total, LAT // TILE)).astype(jnp.bfloat16)
        for h in range(HEADS):
            up = jnp.dot(latent[h * TILE : (h + 1) * TILE], w_ref[h], preferred_element_type=jnp.float32)
            out_ref[h, b * TILE : (b + 1) * TILE, :] = up.astype(jnp.bfloat16)


smem = pl.BlockSpec(memory_space=pltpu.SMEM)
vmem = pl.BlockSpec(memory_space=pltpu.VMEM)


def lay_beside(rows_ref, out_ref):
    rows = rows_ref[...].astype(jnp.float32)
    low, high = rows[:4], rows[4:]
    block = jnp.concatenate([low[:, :LAT], high[:, :LAT], low[:, LAT:], high[:, LAT:]], axis=1).astype(jnp.bfloat16)
    for n in range(16):
        out_ref[n] = block


def beside(rows):
    return pl.pallas_call(
        lay_beside,
        out_shape=jax.ShapeDtypeStruct((16, 4, 2 * KV), jnp.bfloat16),
        in_specs=[vmem],
        out_specs=vmem,
        name="beside",
    )(rows)


def pack(depth, column_ref, block_ref):
    for zh in range(depth):
        rows = jnp.concatenate([column_ref[4 * zh + n].astype(jnp.float32) for n in range(4)], axis=0)
        block = jnp.concatenate([rows[:, n * TILE : (n + 1) * TILE] for n in range(9)], axis=0).astype(jnp.bfloat16)
        for to in range(4):
            block_ref[to, zh] = block


def packed(depth, column):
    return pl.pallas_call(
        functools.partial(pack, depth),
        out_shape=jax.ShapeDtypeStruct((4, depth, 144, TILE), jnp.bfloat16),
        in_specs=[vmem],
        out_specs=vmem,
        name="packed",
    )(column)


part = jax.ShapeDtypeStruct((BLOCKS, HEADS * TILE, TILE), jnp.float32)
accumulated = (jax.ShapeDtypeStruct((BLOCKS, HEADS * TILE, LAT), jnp.float32), part, part)


def own_half(place, plan, q, kv):
    most = min(6, 2 * kv.shape[1])
    pairs = min(OWN_PAIRS, most)
    return pl.pallas_call(
        functools.partial(attend_own, pairs, most > pairs),
        out_shape=(jax.ShapeDtypeStruct((BLOCKS, HEADS * TILE, LAT + TILE), jnp.bfloat16), *accumulated),
        in_specs=[smem, smem, vmem, vmem],
        out_specs=(vmem, vmem, vmem, vmem),
        scratch_shapes=[pltpu.VMEM((2, HEADS * TILE, 2 * pairs * TILE), jnp.float32)],
        compiler_params=pltpu.CompilerParams(vmem_limit_bytes=16 * 1024 * 1024),
        cost_estimate=pl.CostEstimate(flops=1 << 31, bytes_accessed=1 << 22, transcendentals=1 << 20),
        name="own_half",
    )(place, plan, q, kv)


def other_half(place, plan, kv, parts, w):
    most = min(6, 2 * kv.shape[1])
    pairs = min(OTHER_PAIRS, most)
    return pl.pallas_call(
        functools.partial(attend_other, pairs, most > pairs),
        out_shape=jax.ShapeDtypeStruct((HEADS, ROWS, 128), jnp.bfloat16),
        in_specs=[smem, smem, vmem, vmem, vmem, vmem, vmem, vmem],
        out_specs=vmem,
        scratch_shapes=[
            pltpu.VMEM((2, HEADS * TILE, 2 * pairs * TILE), jnp.float32),
            *(pltpu.VMEM(a.shape, a.dtype) for a in accumulated if most > pairs),
        ],
        compiler_params=pltpu.CompilerParams(vmem_limit_bytes=16 * 1024 * 1024),
        cost_estimate=pl.CostEstimate(flops=1 << 31, bytes_accessed=1 << 22, transcendentals=1 << 20),
        name="other_half",
    )(place, plan, kv, *parts, w)


def device_at(zh, core, y, x, zl):
    return (((zh * 2 + core) * 4 + y) * 4 + x) * 4 + zl


def lines(swapped):
    out = []
    for zh in range(4):
        for core in range(2):
            for at in range(4):
                for zl in range(4):
                    along_x = (core == 0) != swapped
                    out.append([device_at(zh, core, *((at, n) if along_x else (n, at)), zl) for n in range(4)])
    return out


def to_all(blocks, groups):
    return lax.all_to_all(blocks, ALL, 0, 0, axis_index_groups=groups)


other_core = [(device_at(a, c, 0, 0, 0) + n, device_at(a, 1 - c, 0, 0, 0) + n) for a in range(4) for c in range(2) for n in range(64)]


def on_device(queries, kv_latent, vert_tiles, slash_offsets, w_uv):
    zh, core = lax.axis_index("zh"), lax.axis_index("core")
    grp_at = (lax.axis_index("y") * 4 + lax.axis_index("x")) * 4 + lax.axis_index("zl")
    place = jnp.stack([zh * 2 + core, core]).astype(jnp.int32)
    column = lax.all_to_all(beside(kv_latent), ("zh", "zl"), 0, 0)
    plan = choice(place, vert_tiles[grp_at], slash_offsets[grp_at])
    turned = queries.transpose(0, 2, 1)

    def plane(depth, column):
        block = to_all(packed(depth, column), lines(False))
        own = to_all(jnp.broadcast_to(block[None], (4, *block.shape)), lines(True)).reshape(16, depth, 144, TILE)
        other = lax.ppermute(own, ALL, other_core)
        parts = own_half(place, plan, turned, own)
        return other_half(place, plan, other, parts, w_uv)

    return lax.switch(zh, [functools.partial(plane, depth) for depth in range(1, 5)], column)


def solution(mesh):
    fine = Mesh(mesh.devices.reshape(4, 2, 4, 4, 4), ALL)
    ctx, grp = ("zh", "core"), ("y", "x", "zl")
    placed = (P(grp, ctx, None), P(ctx + grp, None), P(), P(), P(grp, None, None))
    return jax.shard_map(
        on_device, mesh=fine, in_specs=placed, out_specs=P(grp, ctx, None), check_vma=False
    )
```
